32 devices in a mesh: row: 16 (over z, y, core), col: 2 (over x).
Axes of the slice: x: 2, y: 2, z: 4, core: 2. Of those that a mesh axis runs over, the one named last changes fastest.
Arguments:
- kernel: bfloat16 [1312, 16, 2, 10496], P(None, 'row', 'col'), may hold values from -1 to 8, as said below
Outputs:
- factored: float32 [1312, 16, 2, 10496], P(None, 'row', 'col')
The draws below stay inside these ranges and needn't reach their ends.
Inputs may be any that keep to these rules, and one draw needn't show every extreme that they name: kernel is symmetric (entry i, j equals entry j, i), and its leading 2 * 256 rows and columns form a positive definite matrix.
All inputs are finite; a program needn't handle non-finite values.
Results may differ from the reference program's by a relative error of at most 0.0086.
Values may be sent and summed in bfloat16 or wider, within the bound.
A program may use at most 256 MiB of HBM per device.

```python
import jax
import jax.numpy as jnp
from jax import lax

B = 256
STEPS = 2
N = 20992
N_ROW = 16
N_COL = 2


def draw_kernel(key, part):
    key_noise = jax.random.fold_in(key, 11)
    key_head = jax.random.fold_in(key, 12)
    key_tail = jax.random.fold_in(key, 13)
    noise = jnp.clip(jax.random.normal(key_noise, (N, N), jnp.float32), -4.0, 4.0)
    position = jnp.arange(N)
    head = position < STEPS * B
    both = jnp.logical_and(head[:, None], head[None, :])
    either = jnp.logical_or(head[:, None], head[None, :])
    scale = jnp.where(both, 0.065, jnp.where(either, 0.15, 0.04)).astype(jnp.float32)
    paired = (noise + noise.T) * 0.70710678 * scale
    diag_head = jax.random.uniform(key_head, (N,), jnp.float32, 3.0, 4.0)
    diag_tail = jax.random.uniform(key_tail, (N,), jnp.float32, 5.0, 8.0)
    diagonal = jnp.where(head, diag_head, diag_tail)
    full = jnp.where(position[:, None] == position[None, :], diagonal[:, None], paired)
    return jnp.transpose(full.reshape(N // N_ROW, N_ROW, N // N_COL, N_COL), (0, 1, 3, 2)).astype(jnp.bfloat16)


def setup_inputs(seed: int = 0) -> dict:
    seeds = jax.random.split(jax.random.key(seed), 2)
    return {
        "kernel": draw_kernel(jax.random.fold_in(seeds[1], 71), 0),
    }


def reference(kernel):
    full = jnp.transpose(kernel, (0, 1, 3, 2)).reshape(N, N).astype(jnp.float32)
    eye = jnp.eye(B, dtype=jnp.float32)
    for step in range(STEPS):
        low = step * B
        high = low + B
        rest = N - high
        corner = full[low:high, low:high]
        factor = jnp.linalg.cholesky(corner)
        inverse = jax.scipy.linalg.solve_triangular(factor, eye, lower=True)
        inverse_b = inverse.astype(jnp.bfloat16)
        column_b = full[high:, low:high].astype(jnp.bfloat16)
        solved = lax.dot_general(column_b.astype(jnp.float32), inverse_b.astype(jnp.float32), (((1,), (1,)), ((), ())), preferred_element_type=jnp.float32)
        solved_b = solved.astype(jnp.bfloat16)

        def update_block(index, matrix):
            start = (high + index * B).astype(jnp.int32)
            rows_b = lax.dynamic_slice_in_dim(solved_b, (index * B).astype(jnp.int32), B, 0)
            product = lax.dot_general(rows_b.astype(jnp.float32), solved_b.astype(jnp.float32), (((1,), (1,)), ((), ())), preferred_element_type=jnp.float32)
            current = lax.dynamic_slice(matrix, (start, jnp.int32(high)), (B, rest))
            return lax.dynamic_update_slice(matrix, current - product, (start, jnp.int32(high)))
        full = lax.fori_loop(jnp.int32(0), jnp.int32(rest // B), update_block, full)
        full = full.at[low:high, low:high].set(factor)
        full = full.at[high:, low:high].set(solved)
        full = full.at[low:high, high:].set(solved.T)
    return jnp.transpose(full.reshape(N // N_ROW, N_ROW, N // N_COL, N_COL), (0, 1, 3, 2))
```

```python
import functools

import jax
import jax.numpy as jnp
from jax import lax
from jax.experimental import pallas as pl
from jax.experimental.pallas import tpu as pltpu
from jax.sharding import PartitionSpec as P

B = 256
STEPS = 2
HALF = 128
LANES = 128
ROW_TILE = 272
MIB = 1024 * 1024


def contract_last(left, right):
    return lax.dot_general(
        left, right, (((1,), (1,)), ((), ())), preferred_element_type=jnp.float32
    )


def plain_dot(left, right):
    return jnp.dot(left, right, preferred_element_type=jnp.float32)


def full_dot(left, right, dims=(((1,), (0,)), ((), ()))):
    return lax.dot_general(
        left, right, dims, precision=lax.Precision.HIGHEST, preferred_element_type=jnp.float32
    )


def one_hot(shape, condition):
    i = lax.broadcasted_iota(jnp.int32, shape, 0)
    j = lax.broadcasted_iota(jnp.int32, shape, 1)
    return jnp.where(condition(i, j), 1.0, 0.0)


def eliminate(block):
    groups = HALF // 8
    lane = lax.broadcasted_iota(jnp.int32, (8, LANES), 1)
    sub = lax.broadcasted_iota(jnp.int32, (8, LANES), 0)
    left = [block[8 * g:8 * g + 8, :] for g in range(groups)]
    right = [jnp.where(lane == sub + 8 * g, 1.0, 0.0) for g in range(groups)]
    scale = [jnp.zeros((8, LANES), jnp.float32) for _ in range(groups)]
    for k in range(HALF):
        g, s = divmod(k, 8)
        row_left = jnp.broadcast_to(left[g][s:s + 1, :], (8, LANES))
        row_right = jnp.broadcast_to(right[g][s:s + 1, :], (8, LANES))
        pivot = jnp.broadcast_to(row_left[:, k:k + 1], (8, LANES))
        scale[g] = jnp.where(sub == s, pivot, scale[g])
        inverse = 1.0 / pivot
        row_left = row_left * inverse
        row_right = row_right * inverse
        for u in range(g, groups):
            if u == g and s == 7:
                continue
            column = jnp.broadcast_to(left[u][:, k:k + 1], (8, LANES))
            if u == g:
                column = jnp.where(sub > s, column, 0.0)
            left[u] = left[u] - column * row_left
            right[u] = right[u] - column * row_right
    return jnp.concatenate([right[g] * lax.rsqrt(scale[g]) for g in range(groups)], axis=0)


def factor_kernel(row_count, col_count, where_ref, diag_ref, g_rows_ref, g_cols_ref, u_rows_ref, u_cols_ref,
                  pick_rows_ref, pick_cols_ref, corner_ref, full, work, done, table):
    row_index, col_index = where_ref[0], where_ref[1]
    wide = STEPS * B
    rows_each, cols_each = B // row_count, B // col_count
    rows_two, cols_two = wide // row_count, wide // col_count
    gathered = jnp.concatenate(
        [
            jnp.concatenate([diag_ref[r * col_count + c] for r in range(row_count)], axis=0)
            for c in range(col_count)
        ],
        axis=1,
    )
    to_rows = one_hot(
        (wide, wide), lambda i, j: (i % row_count) * rows_two + i // row_count == j
    ).astype(jnp.bfloat16)
    to_cols = one_hot(
        (wide, wide), lambda i, j: (j % col_count) * cols_two + j // col_count == i
    ).astype(jnp.bfloat16)
    full[...] = plain_dot(plain_dot(to_rows, gathered).astype(jnp.bfloat16), to_cols)
    perm_rows = one_hot(
        (B, B), lambda i, j: (j % rows_each) * row_count + j // rows_each == i
    ).astype(jnp.bfloat16)
    perm_cols = one_hot(
        (B, B), lambda i, j: (j % cols_each) * col_count + j // cols_each == i
    ).astype(jnp.bfloat16)
    own_rows = one_hot(
        (rows_each, B), lambda i, j: i * row_count + row_index == j
    ).astype(jnp.bfloat16)
    own_cols = one_hot(
        (cols_each, B), lambda i, j: i * col_count + col_index == j
    ).astype(jnp.bfloat16)

    @pl.loop(0, STEPS)
    def _(step):
        here = pl.ds(pl.multiple_of(step * B, B), B)
        work[:, :B] = full[here, here]
        work[:, B:] = one_hot((B, B), lambda i, j: i == j)

        @pl.loop(0, B // HALF)
        def _(part):
            strip = pl.ds(pl.multiple_of(part * HALF, HALF), HALF)
            inverse = eliminate(work[strip, strip])
            rows = full_dot(inverse, work[strip, :])
            done[strip, :] = rows

            @pl.when(part == 0)
            def _():
                work[HALF:, :] = work[HALF:, :] - full_dot(
                    rows[:, HALF:B], rows, (((0,), (0,)), ((), ()))
                )

        i = lax.broadcasted_iota(jnp.int32, (B, B), 0)
        j = lax.broadcasted_iota(jnp.int32, (B, B), 1)
        upper = jnp.where(i <= j, done[:, :B], 0.0)
        table[here, here] = upper.T
        inverse_b = done[:, B:].astype(jnp.bfloat16)
        g_rows = plain_dot(inverse_b, perm_rows).astype(jnp.bfloat16)
        g_cols = plain_dot(inverse_b, perm_cols).astype(jnp.bfloat16)
        g_rows_ref[step] = g_rows
        g_cols_ref[step] = g_cols
        pick_rows_ref[step] = plain_dot(own_rows, g_rows).astype(jnp.bfloat16)
        pick_cols_ref[step] = plain_dot(own_cols, g_cols).astype(jnp.bfloat16)

        @pl.when(step == 0)
        def _():
            column_b = full[B:, :B].astype(jnp.bfloat16)
            solved = contract_last(column_b, inverse_b)
            solved_b = solved.astype(jnp.bfloat16)
            table[B:, :B] = solved
            table[:B, B:] = contract_last(inverse_b, column_b)
            full[B:, B:] = full[B:, B:] - contract_last(solved_b, solved_b)
            transposed_in = (((0,), (0,)), ((), ()))
            u_rows_ref[...] = lax.dot_general(
                perm_rows, solved_b, transposed_in, preferred_element_type=jnp.float32
            ).astype(jnp.bfloat16)
            u_cols_ref[...] = lax.dot_general(
                perm_cols, solved_b, transposed_in, preferred_element_type=jnp.float32
            ).astype(jnp.bfloat16)

    mine = one_hot((rows_two, wide), lambda i, j: i * row_count + row_index == j)
    theirs = one_hot((wide, cols_two), lambda i, j: j * col_count + col_index == i)
    corner_ref[...] = full_dot(full_dot(mine, table[...]), theirs)


def factor_call(where, diag, row_count, col_count):
    wide = STEPS * B
    rows_each, cols_each = B // row_count, B // col_count
    shape = jax.ShapeDtypeStruct
    return pl.pallas_call(
        functools.partial(factor_kernel, row_count, col_count),
        out_shape=(
            shape((STEPS, B, B), jnp.bfloat16),
            shape((STEPS, B, B), jnp.bfloat16),
            shape((B, B), jnp.bfloat16),
            shape((B, B), jnp.bfloat16),
            shape((STEPS, rows_each, B), jnp.bfloat16),
            shape((STEPS, cols_each, B), jnp.bfloat16),
            shape((wide // row_count, wide // col_count), jnp.float32),
        ),
        in_specs=[pl.BlockSpec(memory_space=pltpu.SMEM), pl.BlockSpec(memory_space=pltpu.VMEM)],
        out_specs=tuple(pl.BlockSpec(memory_space=pltpu.VMEM) for _ in range(7)),
        scratch_shapes=[
            pltpu.VMEM((wide, wide), jnp.float32),
            pltpu.VMEM((B, 2 * B), jnp.float32),
            pltpu.VMEM((B, 2 * B), jnp.float32),
            pltpu.VMEM((wide, wide), jnp.float32),
        ],
        compiler_params=pltpu.CompilerParams(vmem_limit_bytes=24 * MIB),
        cost_estimate=pl.CostEstimate(flops=60_000_000_000, bytes_accessed=4_000_000, transcendentals=0),
    )(where, diag)


def update_kernel(row_tile, chunk, block_ref, rows_any, column_ref, g_rows_ref, g_cols_ref, u_rows_ref, u_cols_ref,
                  pick_rows_ref, pick_cols_ref, corner_ref, out_ref, panel, top, side, side_b, sem):
    index = pl.program_id(0)
    row_count, rows_two, columns = panel.shape
    col_count = column_ref.shape[0]
    rows_each = rows_two // STEPS
    cols_two = column_ref.shape[2]
    cols_each = cols_two // STEPS
    stride = columns // LANES
    chunks = columns // chunk

    @pl.when(index == 0)
    def _():
        load = pltpu.make_async_copy(rows_any, panel, sem)
        load.start()
        side[...] = jnp.zeros_like(side)
        side_b[...] = jnp.zeros_like(side_b)

        def piece(step):
            return jnp.concatenate(
                [column_ref[c, :, step * cols_each:(step + 1) * cols_each] for c in range(col_count)], axis=1
            )

        first = piece(0)
        solved_b = contract_last(first, g_cols_ref[0]).astype(jnp.bfloat16)
        height = column_ref.shape[1]
        side[:height, :cols_each] = contract_last(first, pick_cols_ref[0])
        side_b[:height, :B] = solved_b
        second = piece(1).astype(jnp.float32) - contract_last(solved_b, u_cols_ref[...])
        second = second.astype(jnp.bfloat16)
        side_b[:height, B:] = contract_last(second, g_cols_ref[1]).astype(jnp.bfloat16)
        side[:height, cols_each:] = contract_last(second, pick_cols_ref[1])
        load.wait()

        @pl.loop(0, chunks)
        def _(at):
            span = pl.ds(pl.multiple_of(at * chunk, chunk), chunk)
            both = panel[:, :, span]
            one = both[:, :rows_each, :].reshape(B, chunk)
            two = both[:, rows_each:, :].reshape(B, chunk)
            solved = plain_dot(g_rows_ref[0], one).astype(jnp.bfloat16)
            top[:rows_each, span] = plain_dot(pick_rows_ref[0], one)
            two = (two.astype(jnp.float32) - plain_dot(u_rows_ref[...], solved)).astype(jnp.bfloat16)
            top[rows_each:, span] = plain_dot(pick_rows_ref[1], two)
            last = plain_dot(g_rows_ref[1], two).astype(jnp.bfloat16)
            panel[:row_count // 2, :, span] = solved.reshape(row_count // 2, rows_two, chunk)
            panel[row_count // 2:, :, span] = last.reshape(row_count // 2, rows_two, chunk)

        top[:, :cols_two] = corner_ref[...]

    rows = pl.ds(pl.multiple_of(index * row_tile, row_tile), row_tile)
    mine = side_b[rows, :]
    first_chunks = cols_two // chunk

    @pl.loop(first_chunks, chunks)
    def _(at):
        span = pl.ds(pl.multiple_of(at * chunk, chunk), chunk)
        other = panel[:, :, span].reshape(STEPS * B, chunk)
        value = block_ref[:, span].astype(jnp.float32) - plain_dot(mine, other)
        for t in range(chunk // LANES):
            out_ref[pl.ds(at * (chunk // LANES) + t, row_tile, stride=stride), :] = value[
                :, t * LANES:(t + 1) * LANES
            ]

    for t in range(cols_two // LANES):
        out_ref[pl.ds(t, row_tile, stride=stride), :] = side[rows, t * LANES:(t + 1) * LANES]

    @pl.when(index == 0)
    def _():
        for t in range(stride):
            out_ref[pl.ds(t, rows_two, stride=stride), :] = top[:, t * LANES:(t + 1) * LANES]


def update_call(block, rows, column, parts, row_tile, chunk):
    height, columns = block.shape
    stride = columns // LANES
    steps = pl.cdiv(height, row_tile)
    whole = pl.BlockSpec(memory_space=pltpu.VMEM)
    return pl.pallas_call(
        functools.partial(update_kernel, row_tile, chunk),
        grid=(steps,),
        out_shape=jax.ShapeDtypeStruct((height * stride, LANES), jnp.float32),
        in_specs=[
            pl.BlockSpec((row_tile, columns), lambda m: (m, 0)),
            pl.BlockSpec(memory_space=pl.ANY),
        ] + [whole] * 8,
        out_specs=pl.BlockSpec((row_tile * stride, LANES), lambda m: (m, 0)),
        scratch_shapes=[
            pltpu.VMEM(rows.shape, jnp.bfloat16),
            pltpu.VMEM((rows.shape[1], columns), jnp.float32),
            pltpu.VMEM((steps * row_tile, column.shape[2]), jnp.float32),
            pltpu.VMEM((steps * row_tile, STEPS * B), jnp.bfloat16),
            pltpu.SemaphoreType.DMA,
        ],
        compiler_params=pltpu.CompilerParams(vmem_limit_bytes=62 * MIB),
        cost_estimate=pl.CostEstimate(
            flops=2 * height * columns * STEPS * B, bytes_accessed=6 * height * columns, transcendentals=0
        ),
    )(block, rows, column, *parts)


def gathered_on_device(kernel):
    row_count = lax.axis_size("row")
    col_count = lax.axis_size("col")
    where = jnp.stack([lax.axis_index("row"), lax.axis_index("col")]).astype(jnp.int32)
    work = kernel[:, 0, 0, :]
    rows_two, cols_two = STEPS * B // row_count, STEPS * B // col_count
    diag = lax.all_gather(work[:rows_two, :cols_two], ("row", "col"), axis=0, tiled=False)
    diag, work = lax.optimization_barrier((diag, work))
    rows = lax.all_gather(work[:rows_two], "row", axis=0, tiled=False)
    column = lax.all_gather(work[:, :cols_two], "col", axis=0, tiled=False)
    parts = factor_call(where, diag, row_count, col_count)
    out = update_call(work, rows, column, parts, ROW_TILE, B)
    return out.reshape(kernel.shape)


def on_device(kernel):
    row_count = lax.axis_size("row")
    col_count = lax.axis_size("col")
    row_index = lax.axis_index("row")
    col_index = lax.axis_index("col")
    rows_each = B // row_count
    cols_each = B // col_count
    work = kernel[:, 0, 0, :].astype(jnp.float32)
    eye = jnp.eye(B, dtype=jnp.float32)
    for step in range(STEPS):
        row_start = step * rows_each
        row_end = row_start + rows_each
        col_start = step * cols_each
        col_end = col_start + cols_each
        piece = work[row_start:row_end, col_start:col_end].reshape(rows_each, 1, cols_each)
        gathered = lax.all_gather(piece, ("row", "col"), axis=1, tiled=True)
        corner = jnp.transpose(
            gathered.reshape(rows_each, row_count, col_count, cols_each), (0, 1, 3, 2)
        ).reshape(B, B)
        factor = jnp.linalg.cholesky(corner)
        inverse_b = jax.scipy.linalg.solve_triangular(factor, eye, lower=True).astype(jnp.bfloat16)
        column_b = work[row_end:, col_start:col_end].astype(jnp.bfloat16)[:, :, None]
        column_all = lax.all_gather(column_b, "col", axis=2, tiled=True).reshape(-1, B)
        solved = contract_last(column_all, inverse_b)
        inverse_cube = inverse_b.reshape(B, rows_each, row_count)
        row_b = work[row_start:row_end, col_end:].astype(jnp.bfloat16)[:, None, :]
        group_rows = lax.all_gather(row_b, "row", axis=1, tiled=True)
        count = group_rows.shape[1]
        block = inverse_cube.reshape(B, rows_each * count)
        transposed = jnp.dot(
            block, group_rows.reshape(rows_each * count, -1), preferred_element_type=jnp.float32
        )
        solved_b = solved.astype(jnp.bfloat16)
        transposed_b = transposed.astype(jnp.bfloat16)
        trailing = work[row_end:, col_end:] - jnp.dot(
            solved_b, transposed_b, preferred_element_type=jnp.float32
        )
        work = work.at[row_end:, col_end:].set(trailing)
        own_rows = lax.dynamic_index_in_dim(
            factor.reshape(rows_each, row_count, cols_each, col_count), row_index, 1, keepdims=False
        )
        own_factor = lax.dynamic_index_in_dim(own_rows, col_index, 2, keepdims=False)
        own_solved = lax.dynamic_index_in_dim(
            solved.reshape(-1, cols_each, col_count), col_index, 2, keepdims=False
        )
        own_transposed = lax.dynamic_index_in_dim(
            transposed.reshape(rows_each, row_count, -1), row_index, 1, keepdims=False
        )
        work = work.at[row_start:row_end, col_start:col_end].set(own_factor)
        work = work.at[row_end:, col_start:col_end].set(own_solved)
        work = work.at[row_start:row_end, col_end:].set(own_transposed)
    return work[:, None, None, :]


def solution(mesh):
    in_specs = (P(None, "row", "col", None),)
    out_specs = P(None, "row", "col", None)
    by_row, by_col = mesh.shape["row"], mesh.shape["col"]

    def run(kernel):
        height, columns = kernel.shape[0], kernel.shape[3]
        fits = (
            (B // by_row) % 16 == 0
            and (B // by_col) % LANES == 0
            and columns % B == 0
            and height % 16 == 0
            and height >= ROW_TILE
        )
        body = gathered_on_device if fits else on_device
        return jax.shard_map(
            body, mesh=mesh, in_specs=in_specs, out_specs=out_specs, check_vma=False
        )(kernel)

    return run
```

```python
import functools

import jax
import jax.numpy as jnp
from jax import lax
from jax.experimental import pallas as pl
from jax.experimental.pallas import tpu as pltpu
from jax.sharding import PartitionSpec as P

B = 256
STEPS = 2
HALF = 128
LANES = 128
ROW_TILE = 272
CHUNK = 1024
MESH = pl.DeviceIdType.MESH
MIB = 1024 * 1024


def contract_last(left, right):
    return lax.dot_general(
        left, right, (((1,), (1,)), ((), ())), preferred_element_type=jnp.float32
    )


def plain_dot(left, right):
    return jnp.dot(left, right, preferred_element_type=jnp.float32)


def full_dot(left, right, dims=(((1,), (0,)), ((), ()))):
    return lax.dot_general(
        left, right, dims, precision=lax.Precision.HIGHEST, preferred_element_type=jnp.float32
    )


def one_hot(shape, condition):
    i = lax.broadcasted_iota(jnp.int32, shape, 0)
    j = lax.broadcasted_iota(jnp.int32, shape, 1)
    return jnp.where(condition(i, j), 1.0, 0.0)


def eliminate(block):
    groups = HALF // 8
    lane = lax.broadcasted_iota(jnp.int32, (8, LANES), 1)
    sub = lax.broadcasted_iota(jnp.int32, (8, LANES), 0)
    left = [block[8 * g:8 * g + 8, :] for g in range(groups)]
    right = [jnp.where(lane == sub + 8 * g, 1.0, 0.0) for g in range(groups)]
    scale = [jnp.zeros((8, LANES), jnp.float32) for _ in range(groups)]
    for k in range(HALF):
        g, s = divmod(k, 8)
        row_left = jnp.broadcast_to(left[g][s:s + 1, :], (8, LANES))
        row_right = jnp.broadcast_to(right[g][s:s + 1, :], (8, LANES))
        pivot = jnp.broadcast_to(row_left[:, k:k + 1], (8, LANES))
        scale[g] = jnp.where(sub == s, pivot, scale[g])
        inverse = 1.0 / pivot
        row_left = row_left * inverse
        row_right = row_right * inverse
        for u in range(g, groups):
            if u == g and s == 7:
                continue
            column = jnp.broadcast_to(left[u][:, k:k + 1], (8, LANES))
            if u == g:
                column = jnp.where(sub > s, column, 0.0)
            left[u] = left[u] - column * row_left
            right[u] = right[u] - column * row_right
    return jnp.concatenate([right[g] * lax.rsqrt(scale[g]) for g in range(groups)], axis=0)


def part_places(row_count, col_count):
    sizes = (
        ("g_rows", STEPS * B),
        ("g_cols", STEPS * B),
        ("u_rows", B),
        ("u_cols", B),
        ("pick_cols", STEPS * B // col_count),
        ("pick_rows", STEPS * B // row_count),
    )
    places, at = {}, 0
    for name, size in sizes:
        places[name] = at
        at += size
    places["end"] = at
    return places


def exchange_kernel(row_count, block_ref, diag_ref, column_ref, local_sem, pair_send, pair_recv, send_sem, recv_sem):
    row, col = lax.axis_index("row"), lax.axis_index("col")
    other = 1 - col
    rows_two, cols_two = diag_ref.shape[2], diag_ref.shape[3]
    barrier = pltpu.get_barrier_semaphore()
    pl.semaphore_signal(barrier, inc=1, device_id=(row, other), device_id_type=MESH)
    for k in range(1, row_count):
        pl.semaphore_signal(
            barrier, inc=1, device_id=(lax.rem(row + k, row_count), col), device_id_type=MESH
        )
    pl.semaphore_wait(barrier, row_count)

    corner = block_ref.at[pl.ds(0, rows_two), pl.ds(0, cols_two)]
    strip = block_ref.at[:, pl.ds(0, cols_two)]
    own_corner = pltpu.make_async_copy(corner, diag_ref.at[row, col], local_sem.at[0])
    own_strip = pltpu.make_async_copy(strip, column_ref.at[col], local_sem.at[1])

    def to_pair(source, target, which):
        return pltpu.make_async_remote_copy(
            src_ref=source,
            dst_ref=target,
            send_sem=pair_send.at[which],
            recv_sem=pair_recv.at[which],
            device_id=(row, other),
            device_id_type=MESH,
        )

    def to_row(slot, k):
        return pltpu.make_async_remote_copy(
            src_ref=diag_ref.at[slot],
            dst_ref=diag_ref.at[slot],
            send_sem=send_sem.at[k],
            recv_sem=recv_sem.at[slot],
            device_id=(lax.rem(row + k, row_count), col),
            device_id_type=MESH,
        )

    small = to_pair(corner, diag_ref.at[row, col], 0)
    large = to_pair(strip, column_ref.at[col], 1)
    small.start()
    own_corner.start()
    own_corner.wait()
    to_pair(corner, diag_ref.at[row, other], 0).wait_recv()
    sends = [to_row(row, k) for k in range(1, row_count)]
    for copy in sends:
        copy.start()
    large.start()
    own_strip.start()
    for k in range(1, row_count):
        to_row(lax.rem(row - k + row_count, row_count), k).wait_recv()
    for copy in sends:
        copy.wait_send()
    to_pair(strip, column_ref.at[other], 1).wait_recv()
    small.wait_send()
    large.wait_send()
    own_strip.wait()


def exchange_call(block, row_count, col_count):
    height = block.shape[0]
    rows_two, cols_two = STEPS * B // row_count, STEPS * B // col_count
    return pl.pallas_call(
        functools.partial(exchange_kernel, row_count),
        out_shape=(
            jax.ShapeDtypeStruct((row_count, col_count, rows_two, cols_two), block.dtype),
            jax.ShapeDtypeStruct((col_count, height, cols_two), block.dtype),
        ),
        in_specs=[pl.BlockSpec(memory_space=pl.ANY)],
        out_specs=(pl.BlockSpec(memory_space=pltpu.VMEM), pl.BlockSpec(memory_space=pl.ANY)),
        scratch_shapes=[
            pltpu.SemaphoreType.DMA((2,)),
            pltpu.SemaphoreType.DMA((2,)),
            pltpu.SemaphoreType.DMA((2,)),
            pltpu.SemaphoreType.DMA((row_count,)),
            pltpu.SemaphoreType.DMA((row_count,)),
        ],
        compiler_params=pltpu.CompilerParams(collective_id=0, has_side_effects=True),
    )(block)


def factor_kernel(row_count, col_count, where_ref, diag_ref, parts_ref, corner_ref, full, work, done, table):
    row_index, col_index = where_ref[0], where_ref[1]
    wide = STEPS * B
    rows_each, cols_each = B // row_count, B // col_count
    rows_two, cols_two = wide // row_count, wide // col_count
    places = part_places(row_count, col_count)
    gathered = jnp.concatenate(
        [
            jnp.concatenate([diag_ref[r, c] for r in range(row_count)], axis=0)
            for c in range(col_count)
        ],
        axis=1,
    )
    to_rows = one_hot(
        (wide, wide), lambda i, j: (i % row_count) * rows_two + i // row_count == j
    ).astype(jnp.bfloat16)
    to_cols = one_hot(
        (wide, wide), lambda i, j: (j % col_count) * cols_two + j // col_count == i
    ).astype(jnp.bfloat16)
    full[...] = plain_dot(plain_dot(to_rows, gathered).astype(jnp.bfloat16), to_cols)
    perm_rows = one_hot(
        (B, B), lambda i, j: (j % rows_each) * row_count + j // rows_each == i
    ).astype(jnp.bfloat16)
    perm_cols = one_hot(
        (B, B), lambda i, j: (j % cols_each) * col_count + j // cols_each == i
    ).astype(jnp.bfloat16)
    own_rows = one_hot(
        (rows_each, B), lambda i, j: i * row_count + row_index == j
    ).astype(jnp.bfloat16)
    own_cols = one_hot(
        (cols_each, B), lambda i, j: i * col_count + col_index == j
    ).astype(jnp.bfloat16)

    @pl.loop(0, STEPS)
    def _(step):
        here = pl.ds(pl.multiple_of(step * B, B), B)
        work[:, :B] = full[here, here]
        work[:, B:] = one_hot((B, B), lambda i, j: i == j)

        @pl.loop(0, B // HALF)
        def _(part):
            strip = pl.ds(pl.multiple_of(part * HALF, HALF), HALF)
            inverse = eliminate(work[strip, strip])
            rows = full_dot(inverse, work[strip, :])
            done[strip, :] = rows

            @pl.when(part == 0)
            def _():
                work[HALF:, :] = work[HALF:, :] - full_dot(
                    rows[:, HALF:B], rows, (((0,), (0,)), ((), ()))
                )

        i = lax.broadcasted_iota(jnp.int32, (B, B), 0)
        j = lax.broadcasted_iota(jnp.int32, (B, B), 1)
        upper = jnp.where(i <= j, done[:, :B], 0.0)
        table[here, here] = upper.T
        inverse_b = done[:, B:].astype(jnp.bfloat16)
        g_rows = plain_dot(inverse_b, perm_rows).astype(jnp.bfloat16)
        g_cols = plain_dot(inverse_b, perm_cols).astype(jnp.bfloat16)

        def place(name, size):
            return pl.ds(pl.multiple_of(places[name] + step * size, 16), size)

        parts_ref[place("g_rows", B), :] = g_rows
        parts_ref[place("g_cols", B), :] = g_cols
        parts_ref[place("pick_rows", rows_each), :] = plain_dot(own_rows, g_rows).astype(jnp.bfloat16)
        parts_ref[place("pick_cols", cols_each), :] = plain_dot(own_cols, g_cols).astype(jnp.bfloat16)

        @pl.when(step == 0)
        def _():
            column_b = full[B:, :B].astype(jnp.bfloat16)
            solved = contract_last(column_b, inverse_b)
            solved_b = solved.astype(jnp.bfloat16)
            table[B:, :B] = solved
            table[:B, B:] = contract_last(inverse_b, column_b)
            full[B:, B:] = full[B:, B:] - contract_last(solved_b, solved_b)
            transposed_in = (((0,), (0,)), ((), ()))
            parts_ref[places["u_rows"]:places["u_rows"] + B, :] = lax.dot_general(
                perm_rows, solved_b, transposed_in, preferred_element_type=jnp.float32
            ).astype(jnp.bfloat16)
            parts_ref[places["u_cols"]:places["u_cols"] + B, :] = lax.dot_general(
                perm_cols, solved_b, transposed_in, preferred_element_type=jnp.float32
            ).astype(jnp.bfloat16)

    mine = one_hot((rows_two, wide), lambda i, j: i * row_count + row_index == j)
    theirs = one_hot((wide, cols_two), lambda i, j: j * col_count + col_index == i)
    corner_ref[...] = full_dot(full_dot(mine, table[...]), theirs)


def factor_call(where, diag, row_count, col_count):
    wide = STEPS * B
    shape = jax.ShapeDtypeStruct
    return pl.pallas_call(
        functools.partial(factor_kernel, row_count, col_count),
        out_shape=(
            shape((part_places(row_count, col_count)["end"], B), jnp.bfloat16),
            shape((wide // row_count, wide // col_count), jnp.float32),
        ),
        in_specs=[pl.BlockSpec(memory_space=pltpu.SMEM), pl.BlockSpec(memory_space=pltpu.VMEM)],
        out_specs=tuple(pl.BlockSpec(memory_space=pltpu.VMEM) for _ in range(2)),
        scratch_shapes=[
            pltpu.VMEM((wide, wide), jnp.float32),
            pltpu.VMEM((B, 2 * B), jnp.float32),
            pltpu.VMEM((B, 2 * B), jnp.float32),
            pltpu.VMEM((wide, wide), jnp.float32),
        ],
        compiler_params=pltpu.CompilerParams(vmem_limit_bytes=24 * MIB),
        cost_estimate=pl.CostEstimate(flops=60_000_000_000, bytes_accessed=4_000_000, transcendentals=0),
    )(where, diag)


def update_kernel(row_tile, places, block_ref, rows_any, column_ref, parts_ref, corner_ref, out_ref, panel, top,
                  side, side_b, sem):
    index = pl.program_id(0)
    row_count, rows_two, columns = panel.shape
    col_count, height, cols_two = column_ref.shape
    rows_each = rows_two // STEPS
    cols_each = cols_two // STEPS
    stride = columns // LANES
    chunks = columns // CHUNK

    def part(name, size, step=0):
        begin = places[name] + step * size
        return parts_ref[begin:begin + size, :]

    def over_columns(body):
        @pl.loop(0, chunks)
        def _(at):
            body(pl.multiple_of(at * CHUNK, CHUNK), CHUNK)

        if columns % CHUNK:
            body(chunks * CHUNK, columns % CHUNK)

    @pl.when(index == 0)
    def _():
        load = pltpu.make_async_copy(rows_any, panel, sem)
        load.start()
        side[...] = jnp.zeros_like(side)
        side_b[...] = jnp.zeros_like(side_b)

        def piece(step):
            return jnp.concatenate(
                [column_ref[c, :, step * cols_each:(step + 1) * cols_each] for c in range(col_count)], axis=1
            )

        first = piece(0)
        solved_b = contract_last(first, part("g_cols", B)).astype(jnp.bfloat16)
        side[:height, :cols_each] = contract_last(first, part("pick_cols", cols_each))
        side_b[:height, :B] = solved_b
        second = piece(1).astype(jnp.float32) - contract_last(solved_b, part("u_cols", B))
        second = second.astype(jnp.bfloat16)
        side_b[:height, B:] = contract_last(second, part("g_cols", B, 1)).astype(jnp.bfloat16)
        side[:height, cols_each:] = contract_last(second, part("pick_cols", cols_each, 1))
        load.wait()

        def solve(start, width):
            span = pl.ds(start, width)
            both = panel[:, :, span]
            one = both[:, :rows_each, :].reshape(B, width)
            two = both[:, rows_each:, :].reshape(B, width)
            solved = plain_dot(part("g_rows", B), one).astype(jnp.bfloat16)
            top[:rows_each, span] = plain_dot(part("pick_rows", rows_each), one)
            two = (two.astype(jnp.float32) - plain_dot(part("u_rows", B), solved)).astype(jnp.bfloat16)
            top[rows_each:, span] = plain_dot(part("pick_rows", rows_each, 1), two)
            last = plain_dot(part("g_rows", B, 1), two).astype(jnp.bfloat16)
            panel[:row_count // 2, :, span] = solved.reshape(row_count // 2, rows_two, width)
            panel[row_count // 2:, :, span] = last.reshape(row_count // 2, rows_two, width)

        over_columns(solve)
        top[:, :cols_two] = corner_ref[...]

    rows = pl.ds(pl.multiple_of(index * row_tile, row_tile), row_tile)

    def subtract(start, width):
        span = pl.ds(start, width)
        other = panel[:, :, span].reshape(STEPS * B, width)
        value = block_ref[:, span].astype(jnp.float32) - plain_dot(side_b[rows, :], other)
        for t in range(width // LANES):
            out_ref[pl.ds(start // LANES + t, row_tile, stride=stride), :] = value[
                :, t * LANES:(t + 1) * LANES
            ]

    over_columns(subtract)
    for t in range(cols_two // LANES):
        out_ref[pl.ds(t, row_tile, stride=stride), :] = side[rows, t * LANES:(t + 1) * LANES]

    @pl.when(index == 0)
    def _():
        for t in range(stride):
            out_ref[pl.ds(t, rows_two, stride=stride), :] = top[:, t * LANES:(t + 1) * LANES]


def update_call(block, rows, column, parts, corner, places, row_tile):
    height, columns = block.shape
    stride = columns // LANES
    steps = pl.cdiv(height, row_tile)
    whole = pl.BlockSpec(memory_space=pltpu.VMEM)
    return pl.pallas_call(
        functools.partial(update_kernel, row_tile, places),
        grid=(steps,),
        out_shape=jax.ShapeDtypeStruct((height * stride, LANES), jnp.float32),
        in_specs=[
            pl.BlockSpec((row_tile, columns), lambda m: (m, 0)),
            pl.BlockSpec(memory_space=pl.ANY),
        ] + [whole] * 3,
        out_specs=pl.BlockSpec((row_tile * stride, LANES), lambda m: (m, 0)),
        scratch_shapes=[
            pltpu.VMEM(rows.shape, jnp.bfloat16),
            pltpu.VMEM((rows.shape[1], columns), jnp.float32),
            pltpu.VMEM((steps * row_tile, column.shape[2]), jnp.float32),
            pltpu.VMEM((steps * row_tile, STEPS * B), jnp.bfloat16),
            pltpu.SemaphoreType.DMA,
        ],
        compiler_params=pltpu.CompilerParams(vmem_limit_bytes=62 * MIB),
        cost_estimate=pl.CostEstimate(
            flops=2 * height * columns * STEPS * B, bytes_accessed=6 * height * columns, transcendentals=0
        ),
    )(block, rows, column, parts, corner)


def gathered_on_device(kernel):
    row_count = lax.axis_size("row")
    col_count = lax.axis_size("col")
    where = jnp.stack([lax.axis_index("row"), lax.axis_index("col")]).astype(jnp.int32)
    work = kernel[:, 0, 0, :]
    rows = lax.all_gather(work[:STEPS * B // row_count], "row", axis=0, tiled=False)
    diag, column = exchange_call(work, row_count, col_count)
    parts, corner = factor_call(where, diag, row_count, col_count)
    out = update_call(work, rows, column, parts, corner, part_places(row_count, col_count), ROW_TILE)
    return out.reshape(kernel.shape)


def on_device(kernel):
    row_count = lax.axis_size("row")
    col_count = lax.axis_size("col")
    row_index = lax.axis_index("row")
    col_index = lax.axis_index("col")
    rows_each = B // row_count
    cols_each = B // col_count
    work = kernel[:, 0, 0, :].astype(jnp.float32)
    eye = jnp.eye(B, dtype=jnp.float32)
    for step in range(STEPS):
        row_start = step * rows_each
        row_end = row_start + rows_each
        col_start = step * cols_each
        col_end = col_start + cols_each
        piece = work[row_start:row_end, col_start:col_end].reshape(rows_each, 1, cols_each)
        gathered = lax.all_gather(piece, ("row", "col"), axis=1, tiled=True)
        corner = jnp.transpose(
            gathered.reshape(rows_each, row_count, col_count, cols_each), (0, 1, 3, 2)
        ).reshape(B, B)
        factor = jnp.linalg.cholesky(corner)
        inverse_b = jax.scipy.linalg.solve_triangular(factor, eye, lower=True).astype(jnp.bfloat16)
        column_b = work[row_end:, col_start:col_end].astype(jnp.bfloat16)[:, :, None]
        column_all = lax.all_gather(column_b, "col", axis=2, tiled=True).reshape(-1, B)
        solved = contract_last(column_all, inverse_b)
        inverse_cube = inverse_b.reshape(B, rows_each, row_count)
        row_b = work[row_start:row_end, col_end:].astype(jnp.bfloat16)[:, None, :]
        group_rows = lax.all_gather(row_b, "row", axis=1, tiled=True)
        count = group_rows.shape[1]
        block = inverse_cube.reshape(B, rows_each * count)
        transposed = jnp.dot(
            block, group_rows.reshape(rows_each * count, -1), preferred_element_type=jnp.float32
        )
        solved_b = solved.astype(jnp.bfloat16)
        transposed_b = transposed.astype(jnp.bfloat16)
        trailing = work[row_end:, col_end:] - jnp.dot(
            solved_b, transposed_b, preferred_element_type=jnp.float32
        )
        work = work.at[row_end:, col_end:].set(trailing)
        own_rows = lax.dynamic_index_in_dim(
            factor.reshape(rows_each, row_count, cols_each, col_count), row_index, 1, keepdims=False
        )
        own_factor = lax.dynamic_index_in_dim(own_rows, col_index, 2, keepdims=False)
        own_solved = lax.dynamic_index_in_dim(
            solved.reshape(-1, cols_each, col_count), col_index, 2, keepdims=False
        )
        own_transposed = lax.dynamic_index_in_dim(
            transposed.reshape(rows_each, row_count, -1), row_index, 1, keepdims=False
        )
        work = work.at[row_start:row_end, col_start:col_end].set(own_factor)
        work = work.at[row_end:, col_start:col_end].set(own_solved)
        work = work.at[row_start:row_end, col_end:].set(own_transposed)
    return work[:, None, None, :]


def solution(mesh):
    in_specs = (P(None, "row", "col", None),)
    out_specs = P(None, "row", "col", None)
    by_row, by_col = mesh.shape["row"], mesh.shape["col"]

    def run(kernel):
        height, columns = kernel.shape[0], kernel.shape[3]
        fits = (
            (B // by_row) % 16 == 0
            and (B // by_col) % LANES == 0
            and by_col == 2
            and columns % B == 0
            and height % 16 == 0
            and height >= ROW_TILE
        )
        body = gathered_on_device if fits else on_device
        return jax.shard_map(
            body, mesh=mesh, in_specs=in_specs, out_specs=out_specs, check_vma=False
        )(kernel)

    return run
```

```python
import functools

import jax
import jax.numpy as jnp
from jax import lax
from jax.experimental import pallas as pl
from jax.experimental.pallas import tpu as pltpu
from jax.sharding import PartitionSpec as P

B = 256
STEPS = 2
HALF = 128
LANES = 128
ROW_TILE = 272
CHUNK = 1024
MESH = pl.DeviceIdType.MESH
MIB = 1024 * 1024


def contract_last(left, right):
    return lax.dot_general(
        left, right, (((1,), (1,)), ((), ())), preferred_element_type=jnp.float32
    )


def plain_dot(left, right):
    return jnp.dot(left, right, preferred_element_type=jnp.float32)


def full_dot(left, right, dims=(((1,), (0,)), ((), ()))):
    return lax.dot_general(
        left, right, dims, precision=lax.Precision.HIGHEST, preferred_element_type=jnp.float32
    )


def one_hot(shape, condition):
    i = lax.broadcasted_iota(jnp.int32, shape, 0)
    j = lax.broadcasted_iota(jnp.int32, shape, 1)
    return jnp.where(condition(i, j), 1.0, 0.0)


def eliminate(block):
    groups = HALF // 8
    lane = lax.broadcasted_iota(jnp.int32, (8, LANES), 1)
    sub = lax.broadcasted_iota(jnp.int32, (8, LANES), 0)
    left = [block[8 * g:8 * g + 8, :] for g in range(groups)]
    right = [jnp.where(lane == sub + 8 * g, 1.0, 0.0) for g in range(groups)]
    scale = [jnp.zeros((8, LANES), jnp.float32) for _ in range(groups)]
    for k in range(0, HALF, 2):
        g, s = divmod(k, 8)
        row_left = jnp.broadcast_to(left[g][s:s + 1, :], (8, LANES))
        row_right = jnp.broadcast_to(right[g][s:s + 1, :], (8, LANES))
        next_left = jnp.broadcast_to(left[g][s + 1:s + 2, :], (8, LANES))
        next_right = jnp.broadcast_to(right[g][s + 1:s + 2, :], (8, LANES))
        pivot = jnp.broadcast_to(row_left[:, k:k + 1], (8, LANES))
        cross = jnp.broadcast_to(next_left[:, k:k + 1], (8, LANES))
        corner = jnp.broadcast_to(next_left[:, k + 1:k + 2], (8, LANES))
        inverse = 1.0 / pivot
        ratio = cross * inverse
        second = corner - cross * ratio
        inverse_second = 1.0 / second
        scale[g] = jnp.where(sub == s, pivot, jnp.where(sub == s + 1, second, scale[g]))
        next_left = (next_left - ratio * row_left) * inverse_second
        next_right = (next_right - ratio * row_right) * inverse_second
        row_left = row_left * inverse
        row_right = row_right * inverse
        for u in range(g, groups):
            column = jnp.broadcast_to(left[u][:, k:k + 1], (8, LANES))
            following = jnp.broadcast_to(left[u][:, k + 1:k + 2], (8, LANES)) - column * ratio
            if u == g:
                column = jnp.where(sub > s, column, 0.0)
                following = jnp.where(sub > s + 1, following, 0.0)
            left[u] = left[u] - column * row_left - following * next_left
            right[u] = right[u] - column * row_right - following * next_right
    return jnp.concatenate([right[g] * lax.rsqrt(scale[g]) for g in range(groups)], axis=0)


def part_places(row_count, col_count):
    sizes = (
        ("g_rows", STEPS * B),
        ("g_cols", STEPS * B),
        ("u_rows", B),
        ("u_cols", B),
        ("pick_cols", STEPS * B // col_count),
        ("pick_rows", STEPS * B // row_count),
    )
    places, at = {}, 0
    for name, size in sizes:
        places[name] = at
        at += size
    places["end"] = at
    return places


def exchange_kernel(row_count, block_ref, diag_ref, column_ref, local_sem, pair_send, pair_recv, send_sem, recv_sem):
    row, col = lax.axis_index("row"), lax.axis_index("col")
    other = 1 - col
    rows_two, cols_two = diag_ref.shape[2], diag_ref.shape[3]
    barrier = pltpu.get_barrier_semaphore()
    pl.semaphore_signal(barrier, inc=1, device_id=(row, other), device_id_type=MESH)
    for k in range(1, row_count):
        pl.semaphore_signal(
            barrier, inc=1, device_id=(lax.rem(row + k, row_count), col), device_id_type=MESH
        )
    pl.semaphore_wait(barrier, row_count)

    corner = block_ref.at[pl.ds(0, rows_two), pl.ds(0, cols_two)]
    strip = block_ref.at[:, pl.ds(0, cols_two)]
    own_corner = pltpu.make_async_copy(corner, diag_ref.at[row, col], local_sem.at[0])
    own_strip = pltpu.make_async_copy(strip, column_ref.at[col], local_sem.at[1])

    def to_pair(source, target, which):
        return pltpu.make_async_remote_copy(
            src_ref=source,
            dst_ref=target,
            send_sem=pair_send.at[which],
            recv_sem=pair_recv.at[which],
            device_id=(row, other),
            device_id_type=MESH,
        )

    def to_row(slot, k):
        return pltpu.make_async_remote_copy(
            src_ref=diag_ref.at[slot],
            dst_ref=diag_ref.at[slot],
            send_sem=send_sem.at[k],
            recv_sem=recv_sem.at[slot],
            device_id=(lax.rem(row + k, row_count), col),
            device_id_type=MESH,
        )

    small = to_pair(corner, diag_ref.at[row, col], 0)
    large = to_pair(strip, column_ref.at[col], 1)
    small.start()
    own_corner.start()
    own_corner.wait()
    to_pair(corner, diag_ref.at[row, other], 0).wait_recv()
    sends = [to_row(row, k) for k in range(1, row_count)]
    for copy in sends:
        copy.start()
    large.start()
    own_strip.start()
    for k in range(1, row_count):
        to_row(lax.rem(row - k + row_count, row_count), k).wait_recv()
    for copy in sends:
        copy.wait_send()
    to_pair(strip, column_ref.at[other], 1).wait_recv()
    small.wait_send()
    large.wait_send()
    own_strip.wait()


def exchange_call(block, row_count, col_count):
    height = block.shape[0]
    rows_two, cols_two = STEPS * B // row_count, STEPS * B // col_count
    return pl.pallas_call(
        functools.partial(exchange_kernel, row_count),
        out_shape=(
            jax.ShapeDtypeStruct((row_count, col_count, rows_two, cols_two), block.dtype),
            jax.ShapeDtypeStruct((col_count, height, cols_two), block.dtype),
        ),
        in_specs=[pl.BlockSpec(memory_space=pl.ANY)],
        out_specs=(pl.BlockSpec(memory_space=pltpu.VMEM), pl.BlockSpec(memory_space=pl.ANY)),
        scratch_shapes=[
            pltpu.SemaphoreType.DMA((2,)),
            pltpu.SemaphoreType.DMA((2,)),
            pltpu.SemaphoreType.DMA((2,)),
            pltpu.SemaphoreType.DMA((row_count,)),
            pltpu.SemaphoreType.DMA((row_count,)),
        ],
        compiler_params=pltpu.CompilerParams(collective_id=0, has_side_effects=True),
    )(block)


def factor_kernel(row_count, col_count, where_ref, diag_ref, parts_ref, corner_ref, full, work, done, table):
    row_index, col_index = where_ref[0], where_ref[1]
    wide = STEPS * B
    rows_each, cols_each = B // row_count, B // col_count
    rows_two, cols_two = wide // row_count, wide // col_count
    places = part_places(row_count, col_count)
    gathered = jnp.concatenate(
        [
            jnp.concatenate([diag_ref[r, c] for r in range(row_count)], axis=0)
            for c in range(col_count)
        ],
        axis=1,
    )
    to_rows = one_hot(
        (wide, wide), lambda i, j: (i % row_count) * rows_two + i // row_count == j
    ).astype(jnp.bfloat16)
    to_cols = one_hot(
        (wide, wide), lambda i, j: (j % col_count) * cols_two + j // col_count == i
    ).astype(jnp.bfloat16)
    full[...] = plain_dot(plain_dot(to_rows, gathered).astype(jnp.bfloat16), to_cols)
    perm_rows = one_hot(
        (B, B), lambda i, j: (j % rows_each) * row_count + j // rows_each == i
    ).astype(jnp.bfloat16)
    perm_cols = one_hot(
        (B, B), lambda i, j: (j % cols_each) * col_count + j // cols_each == i
    ).astype(jnp.bfloat16)
    own_rows = one_hot(
        (rows_each, B), lambda i, j: i * row_count + row_index == j
    ).astype(jnp.bfloat16)
    own_cols = one_hot(
        (cols_each, B), lambda i, j: i * col_count + col_index == j
    ).astype(jnp.bfloat16)

    @pl.loop(0, STEPS)
    def _(step):
        here = pl.ds(pl.multiple_of(step * B, B), B)
        work[:, :B] = full[here, here]
        work[:, B:] = one_hot((B, B), lambda i, j: i == j)

        @pl.loop(0, B // HALF)
        def _(part):
            strip = pl.ds(pl.multiple_of(part * HALF, HALF), HALF)
            inverse = eliminate(work[strip, strip])
            rows = full_dot(inverse, work[strip, :])
            done[strip, :] = rows

            @pl.when(part == 0)
            def _():
                work[HALF:, :] = work[HALF:, :] - full_dot(
                    rows[:, HALF:B], rows, (((0,), (0,)), ((), ()))
                )

        i = lax.broadcasted_iota(jnp.int32, (B, B), 0)
        j = lax.broadcasted_iota(jnp.int32, (B, B), 1)
        upper = jnp.where(i <= j, done[:, :B], 0.0)
        table[here, here] = upper.T
        inverse_b = done[:, B:].astype(jnp.bfloat16)
        g_rows = plain_dot(inverse_b, perm_rows).astype(jnp.bfloat16)
        g_cols = plain_dot(inverse_b, perm_cols).astype(jnp.bfloat16)

        def place(name, size):
            return pl.ds(pl.multiple_of(places[name] + step * size, 16), size)

        parts_ref[place("g_rows", B), :] = g_rows
        parts_ref[place("g_cols", B), :] = g_cols
        parts_ref[place("pick_rows", rows_each), :] = plain_dot(own_rows, g_rows).astype(jnp.bfloat16)
        parts_ref[place("pick_cols", cols_each), :] = plain_dot(own_cols, g_cols).astype(jnp.bfloat16)

        @pl.when(step == 0)
        def _():
            column_b = full[B:, :B].astype(jnp.bfloat16)
            solved = contract_last(column_b, inverse_b)
            solved_b = solved.astype(jnp.bfloat16)
            table[B:, :B] = solved
            table[:B, B:] = contract_last(inverse_b, column_b)
            full[B:, B:] = full[B:, B:] - contract_last(solved_b, solved_b)
            transposed_in = (((0,), (0,)), ((), ()))
            parts_ref[places["u_rows"]:places["u_rows"] + B, :] = lax.dot_general(
                perm_rows, solved_b, transposed_in, preferred_element_type=jnp.float32
            ).astype(jnp.bfloat16)
            parts_ref[places["u_cols"]:places["u_cols"] + B, :] = lax.dot_general(
                perm_cols, solved_b, transposed_in, preferred_element_type=jnp.float32
            ).astype(jnp.bfloat16)

    mine = one_hot((rows_two, wide), lambda i, j: i * row_count + row_index == j)
    theirs = one_hot((wide, cols_two), lambda i, j: j * col_count + col_index == i)
    corner_ref[...] = full_dot(full_dot(mine, table[...]), theirs)


def factor_call(where, diag, row_count, col_count):
    wide = STEPS * B
    shape = jax.ShapeDtypeStruct
    return pl.pallas_call(
        functools.partial(factor_kernel, row_count, col_count),
        out_shape=(
            shape((part_places(row_count, col_count)["end"], B), jnp.bfloat16),
            shape((wide // row_count, wide // col_count), jnp.float32),
        ),
        in_specs=[pl.BlockSpec(memory_space=pltpu.SMEM), pl.BlockSpec(memory_space=pltpu.VMEM)],
        out_specs=tuple(pl.BlockSpec(memory_space=pltpu.VMEM) for _ in range(2)),
        scratch_shapes=[
            pltpu.VMEM((wide, wide), jnp.float32),
            pltpu.VMEM((B, 2 * B), jnp.float32),
            pltpu.VMEM((B, 2 * B), jnp.float32),
            pltpu.VMEM((wide, wide), jnp.float32),
        ],
        compiler_params=pltpu.CompilerParams(vmem_limit_bytes=24 * MIB),
        cost_estimate=pl.CostEstimate(flops=60_000_000_000, bytes_accessed=4_000_000, transcendentals=0),
    )(where, diag)


def side_kernel(places, column_ref, parts_ref, side_ref, side_b_ref):
    col_count, height, cols_two = column_ref.shape
    cols_each = cols_two // STEPS

    def part(name, size, step=0):
        begin = places[name] + step * size
        return parts_ref[begin:begin + size, :]

    def piece(step):
        return jnp.concatenate(
            [column_ref[c, :, step * cols_each:(step + 1) * cols_each] for c in range(col_count)], axis=1
        )

    side_ref[...] = jnp.zeros_like(side_ref)
    side_b_ref[...] = jnp.zeros_like(side_b_ref)
    first = piece(0)
    solved_b = contract_last(first, part("g_cols", B)).astype(jnp.bfloat16)
    side_ref[:height, :cols_each] = contract_last(first, part("pick_cols", cols_each))
    side_b_ref[:height, :B] = solved_b
    second = piece(1).astype(jnp.float32) - contract_last(solved_b, part("u_cols", B))
    second = second.astype(jnp.bfloat16)
    side_b_ref[:height, B:] = contract_last(second, part("g_cols", B, 1)).astype(jnp.bfloat16)
    side_ref[:height, cols_each:] = contract_last(second, part("pick_cols", cols_each, 1))


def side_call(column, parts, places, row_tile):
    height = pl.cdiv(column.shape[1], row_tile) * row_tile
    return pl.pallas_call(
        functools.partial(side_kernel, places),
        out_shape=(
            jax.ShapeDtypeStruct((height, column.shape[2]), jnp.float32),
            jax.ShapeDtypeStruct((height, STEPS * B), jnp.bfloat16),
        ),
        in_specs=[pl.BlockSpec(memory_space=pltpu.VMEM)] * 2,
        out_specs=(pl.BlockSpec(memory_space=pltpu.VMEM),) * 2,
        compiler_params=pltpu.CompilerParams(vmem_limit_bytes=32 * MIB),
        cost_estimate=pl.CostEstimate(flops=6_000_000_000, bytes_accessed=8_000_000, transcendentals=0),
    )(column, parts)


def update_kernel(row_tile, places, block_ref, rows_any, side_ref, side_b_ref, parts_ref, corner_ref, out_ref, panel,
                  top, sem):
    index = pl.program_id(0)
    row_count, rows_two, columns = panel.shape
    cols_two = side_ref.shape[1]
    rows_each = rows_two // STEPS
    stride = columns // LANES
    chunks = columns // CHUNK

    def part(name, size, step=0):
        begin = places[name] + step * size
        return parts_ref[begin:begin + size, :]

    def over_columns(body):
        @pl.loop(0, chunks)
        def _(at):
            body(at, pl.multiple_of(at * CHUNK, CHUNK), CHUNK)

        if columns % CHUNK:
            body(chunks, chunks * CHUNK, columns % CHUNK)

    @pl.when(index == 0)
    def _():
        def load(at, start, width):
            span = pl.ds(start, width)
            return pltpu.make_async_copy(rows_any.at[:, :, span], panel.at[:, :, span], sem.at[at])

        def begin(at, start, width):
            load(at, start, width).start()

        over_columns(begin)

        def solve(at, start, width):
            load(at, start, width).wait()
            span = pl.ds(start, width)
            both = panel[:, :, span]
            one = both[:, :rows_each, :].reshape(B, width)
            two = both[:, rows_each:, :].reshape(B, width)
            solved = plain_dot(part("g_rows", B), one).astype(jnp.bfloat16)
            top[:rows_each, span] = plain_dot(part("pick_rows", rows_each), one)
            two = (two.astype(jnp.float32) - plain_dot(part("u_rows", B), solved)).astype(jnp.bfloat16)
            top[rows_each:, span] = plain_dot(part("pick_rows", rows_each, 1), two)
            last = plain_dot(part("g_rows", B, 1), two).astype(jnp.bfloat16)
            panel[:row_count // 2, :, span] = solved.reshape(row_count // 2, rows_two, width)
            panel[row_count // 2:, :, span] = last.reshape(row_count // 2, rows_two, width)

        over_columns(solve)
        top[:, :cols_two] = corner_ref[...]

    def subtract(at, start, width):
        span = pl.ds(start, width)
        other = panel[:, :, span].reshape(STEPS * B, width)
        value = block_ref[:, span].astype(jnp.float32) - plain_dot(side_b_ref[...], other)
        for t in range(width // LANES):
            out_ref[pl.ds(start // LANES + t, row_tile, stride=stride), :] = value[
                :, t * LANES:(t + 1) * LANES
            ]

    over_columns(subtract)
    for t in range(cols_two // LANES):
        out_ref[pl.ds(t, row_tile, stride=stride), :] = side_ref[:, t * LANES:(t + 1) * LANES]

    @pl.when(index == 0)
    def _():
        for t in range(stride):
            out_ref[pl.ds(t, rows_two, stride=stride), :] = top[:, t * LANES:(t + 1) * LANES]


def update_call(block, rows, side, side_b, parts, corner, places, row_tile):
    height, columns = block.shape
    stride = columns // LANES
    steps = pl.cdiv(height, row_tile)
    whole = pl.BlockSpec(memory_space=pltpu.VMEM)
    return pl.pallas_call(
        functools.partial(update_kernel, row_tile, places),
        grid=(steps,),
        out_shape=jax.ShapeDtypeStruct((height * stride, LANES), jnp.float32),
        in_specs=[
            pl.BlockSpec((row_tile, columns), lambda m: (m, 0)),
            pl.BlockSpec(memory_space=pl.ANY),
            pl.BlockSpec((row_tile, side.shape[1]), lambda m: (m, 0)),
            pl.BlockSpec((row_tile, side_b.shape[1]), lambda m: (m, 0)),
            whole,
            whole,
        ],
        out_specs=pl.BlockSpec((row_tile * stride, LANES), lambda m: (m, 0)),
        scratch_shapes=[
            pltpu.VMEM(rows.shape, jnp.bfloat16),
            pltpu.VMEM((rows.shape[1], columns), jnp.float32),
            pltpu.SemaphoreType.DMA((pl.cdiv(columns, CHUNK),)),
        ],
        compiler_params=pltpu.CompilerParams(vmem_limit_bytes=62 * MIB),
        cost_estimate=pl.CostEstimate(
            flops=2 * height * columns * STEPS * B, bytes_accessed=6 * height * columns, transcendentals=0
        ),
    )(block, rows, side, side_b, parts, corner)


def gathered_on_device(kernel):
    row_count = lax.axis_size("row")
    col_count = lax.axis_size("col")
    where = jnp.stack([lax.axis_index("row"), lax.axis_index("col")]).astype(jnp.int32)
    work = kernel[:, 0, 0, :]
    rows = lax.all_gather(work[:STEPS * B // row_count], "row", axis=0, tiled=False)
    diag, column = exchange_call(work, row_count, col_count)
    parts, corner = factor_call(where, diag, row_count, col_count)
    places = part_places(row_count, col_count)
    side, side_b = side_call(column, parts, places, ROW_TILE)
    out = update_call(work, rows, side, side_b, parts, corner, places, ROW_TILE)
    return out.reshape(kernel.shape)


def on_device(kernel):
    row_count = lax.axis_size("row")
    col_count = lax.axis_size("col")
    row_index = lax.axis_index("row")
    col_index = lax.axis_index("col")
    rows_each = B // row_count
    cols_each = B // col_count
    work = kernel[:, 0, 0, :].astype(jnp.float32)
    eye = jnp.eye(B, dtype=jnp.float32)
    for step in range(STEPS):
        row_start = step * rows_each
        row_end = row_start + rows_each
        col_start = step * cols_each
        col_end = col_start + cols_each
        piece = work[row_start:row_end, col_start:col_end].reshape(rows_each, 1, cols_each)
        gathered = lax.all_gather(piece, ("row", "col"), axis=1, tiled=True)
        corner = jnp.transpose(
            gathered.reshape(rows_each, row_count, col_count, cols_each), (0, 1, 3, 2)
        ).reshape(B, B)
        factor = jnp.linalg.cholesky(corner)
        inverse_b = jax.scipy.linalg.solve_triangular(factor, eye, lower=True).astype(jnp.bfloat16)
        column_b = work[row_end:, col_start:col_end].astype(jnp.bfloat16)[:, :, None]
        column_all = lax.all_gather(column_b, "col", axis=2, tiled=True).reshape(-1, B)
        solved = contract_last(column_all, inverse_b)
        inverse_cube = inverse_b.reshape(B, rows_each, row_count)
        row_b = work[row_start:row_end, col_end:].astype(jnp.bfloat16)[:, None, :]
        group_rows = lax.all_gather(row_b, "row", axis=1, tiled=True)
        count = group_rows.shape[1]
        block = inverse_cube.reshape(B, rows_each * count)
        transposed = jnp.dot(
            block, group_rows.reshape(rows_each * count, -1), preferred_element_type=jnp.float32
        )
        solved_b = solved.astype(jnp.bfloat16)
        transposed_b = transposed.astype(jnp.bfloat16)
        trailing = work[row_end:, col_end:] - jnp.dot(
            solved_b, transposed_b, preferred_element_type=jnp.float32
        )
        work = work.at[row_end:, col_end:].set(trailing)
        own_rows = lax.dynamic_index_in_dim(
            factor.reshape(rows_each, row_count, cols_each, col_count), row_index, 1, keepdims=False
        )
        own_factor = lax.dynamic_index_in_dim(own_rows, col_index, 2, keepdims=False)
        own_solved = lax.dynamic_index_in_dim(
            solved.reshape(-1, cols_each, col_count), col_index, 2, keepdims=False
        )
        own_transposed = lax.dynamic_index_in_dim(
            transposed.reshape(rows_each, row_count, -1), row_index, 1, keepdims=False
        )
        work = work.at[row_start:row_end, col_start:col_end].set(own_factor)
        work = work.at[row_end:, col_start:col_end].set(own_solved)
        work = work.at[row_start:row_end, col_end:].set(own_transposed)
    return work[:, None, None, :]


def solution(mesh):
    in_specs = (P(None, "row", "col", None),)
    out_specs = P(None, "row", "col", None)
    by_row, by_col = mesh.shape["row"], mesh.shape["col"]

    def run(kernel):
        height, columns = kernel.shape[0], kernel.shape[3]
        fits = (
            (B // by_row) % 16 == 0
            and (B // by_col) % LANES == 0
            and by_col == 2
            and columns % B == 0
            and height % 16 == 0
            and height >= ROW_TILE
        )
        body = gathered_on_device if fits else on_device
        return jax.shard_map(
            body, mesh=mesh, in_specs=in_specs, out_specs=out_specs, check_vma=False
        )(kernel)

    return run
```
